32 devices in a mesh: groups: 2 (over y), depth: 4 (over z), row: 2 (over x), col: 2 (over core).
Axes of the slice: x: 2, y: 2, z: 4, core: 2. Of those that a mesh axis runs over, the one named last changes fastest.
Arguments:
- voxels: float32 [32, 8, 4, 8, 512], P('depth', None, None, 'col', ('groups', 'row')), parts along dimension 4, may hold values from -6 to 6
- counts: int32 [4, 4, 8, 512], P('depth', None, 'col', ('groups', 'row')), parts along dimension 3, may hold values from 1 to 8, as said below
- ray_order: int32 [4, 128], P(('groups', 'row')), parts along dimension 0, may hold values from 0 to 127, each once within a row
- weight_in: float32 [8, 128], replicated, may hold values from -2 to 2
- bias_in: float32 [128], replicated, may hold values from -3 to 3
- weight_out: float32 [128, 33], replicated, may hold values from -0.5 to 0.5
- bias_out: float32 [33], replicated, may hold values from -3 to 3
- kernel_first: float32 [3, 3, 64, 32], replicated, may hold values from -1 to 1
- bias_first: float32 [64], replicated, may hold values from -2 to 2
- kernel_second: float32 [3, 3, 64, 64], replicated, may hold values from -0.375 to 0.375
- bias_second: float32 [64], replicated, may hold values from -2 to 2
Outputs:
- decoded: float32 [64, 32, 512], P(None, ('depth', 'col'), ('groups', 'row')), parts along dimension 2
The draws below stay inside these ranges and needn't reach their ends.
There are 2 independent parts, one for each index of `groups`. The reference program is written for one: setup_inputs(seed, part) draws one part's arguments, and reference() takes and returns one part's arrays. A program takes and returns all parts, laid end to end along the dimension named above; an argument that names none is the same for every part. Nothing has to cross between parts.
Inputs may be any that keep to these rules, and one draw needn't show every extreme that they name: occupied sample counts; the middle slab (slab 4 // 2) is busy and the slabs far from it hold few occupied samples.
All inputs are finite; a program needn't handle non-finite values.
Results may differ from the reference program's by a relative error of at most 0.0003.
Values sent between devices are 32-bit elements; how exact they have to be, the bound alone decides.
A program may use at most 64 MiB of HBM per device.

```python
import jax
import jax.numpy as jnp
from jax import lax

SL = 8
CW = 4
HB = 128
CH = 8
HID = 128
FEAT = 32
DEC = 64
S = 32
H = 256
N_DEPTH = 4
N_ROW = 2
N_COL = 2


def draw_counts(key, part):
    key = jax.random.fold_in(key, 7)
    shape_all = (N_DEPTH, N_DEPTH, N_COL * CW, N_ROW * HB)
    base = jax.random.randint(key, shape_all, 0, SL + 1)
    middle = N_DEPTH // 2
    slab_index = jnp.arange(N_DEPTH, dtype=jnp.int32)
    distance = jnp.abs(slab_index - middle)
    offset = SL // 2 - SL * distance // max(middle, 1)
    result = jnp.clip(base + offset[:, None, None, None], 1, SL)
    result = result.at[middle, 0, 0, 0].set(SL)
    return result.astype(jnp.int32)


def block_levels(rng, shape, pieces, low, largest):
    def one(axis_at, parts):
        heights = jax.random.uniform(jax.random.fold_in(jax.random.fold_in(rng, 6), axis_at), (parts,), jnp.float32, low / len(pieces), largest / len(pieces))
        return jnp.repeat(jnp.exp(heights), shape[axis_at] // parts).reshape((-1,) + (1,) * (len(shape) - axis_at - 1))

    loudness = one(*pieces[0])
    for cut in pieces[1:]:
        loudness = loudness * one(*cut)
    return loudness


def gaussian(rng, extent, width, bound, pieces=(), kind=jnp.bfloat16):
    drawn = width * jax.random.normal(rng, extent, jnp.float32)
    if pieces:
        drawn = drawn * block_levels(rng, extent, pieces, -0.22, 0.18)
    return jnp.clip(drawn, -bound, bound).astype(kind)


def setup_inputs(seed: int = 0, part: int = 0) -> dict:
    arg_keys = jax.random.split(jax.random.key(seed), 12)
    own_keys = jax.random.split(jax.random.fold_in(arg_keys[11], part), 12)
    voxels = gaussian(own_keys[0], (S, CH, N_DEPTH, N_COL * CW, H), 1.0, 6.0, ((0, 4), (3, 2), (4, 2)), jnp.float32)
    counts = draw_counts(jax.random.fold_in(jax.random.fold_in(arg_keys[11], part), 71), part)
    ray_order = jax.vmap(lambda own: jax.random.permutation(own, HB))(jax.random.split(own_keys[2], N_ROW)).reshape((N_ROW, HB)).astype(jnp.int32)
    weight_in = gaussian(arg_keys[3], (CH, HID), CH ** -0.5, 2.0, (), jnp.float32)
    bias_in = gaussian(arg_keys[4], (HID,), 0.5, 3.0, (), jnp.float32)
    weight_out = gaussian(arg_keys[5], (HID, FEAT + 1), HID ** -0.5, 0.5, (), jnp.float32)
    bias_out = gaussian(arg_keys[6], (FEAT + 1,), 0.5, 3.0, (), jnp.float32)
    kernel_first = gaussian(arg_keys[7], (3, 3, DEC, FEAT), FEAT ** -0.5, 1.0, (), jnp.float32)
    bias_first = gaussian(arg_keys[8], (DEC,), 0.3, 2.0, (), jnp.float32)
    kernel_second = gaussian(arg_keys[9], (3, 3, DEC, DEC), (9 * DEC // 2) ** -0.5, 0.375, (), jnp.float32)
    bias_second = gaussian(arg_keys[10], (DEC,), 0.3, 2.0, (), jnp.float32)
    return dict(voxels=voxels, counts=counts, ray_order=ray_order, weight_in=weight_in, bias_in=bias_in, weight_out=weight_out, bias_out=bias_out, kernel_first=kernel_first, bias_first=bias_first, kernel_second=kernel_second, bias_second=bias_second)


def convolve(field, kernel, bias):
    col_count = field.shape[1]
    row_count = field.shape[2]
    padded = jnp.pad(field, ((0, 0), (1, 1), (1, 1)))
    total = jnp.zeros((kernel.shape[2], col_count, row_count), jnp.float32) + bias[:, None, None]
    for shift_a in range(3):
        for shift_b in range(3):
            window = padded[:, shift_a:shift_a + col_count, shift_b:shift_b + row_count]
            total = total + jnp.einsum("oc,cwh->owh", kernel[shift_a, shift_b], window, precision=lax.Precision.HIGHEST)
    return total


def reference(voxels, counts, ray_order, weight_in, bias_in, weight_out, bias_out, kernel_first, bias_first, kernel_second, bias_second):
    total_samples = SL * N_DEPTH
    image_cols = N_DEPTH * N_COL * CW
    image_rows = N_ROW * HB
    ray_count = image_cols * image_rows
    flat_voxels = voxels.reshape(total_samples, CH, ray_count)
    flat_counts = counts.reshape(N_DEPTH, ray_count)
    step_size = 2.0 / total_samples

    def sample_step(carry, index):
        contrib, depth_sum = carry
        sample_voxels = lax.dynamic_index_in_dim(flat_voxels, index, 0, keepdims=False)
        slab_counts = lax.dynamic_index_in_dim(flat_counts, index // SL, 0, keepdims=False)
        occupied = (slab_counts > index % SL).astype(jnp.float32)
        hidden = jax.nn.relu(jnp.dot(weight_in.T, sample_voxels, precision=lax.Precision.HIGHEST, preferred_element_type=jnp.float32) + bias_in[:, None])
        raw_out = jnp.dot(weight_out.T, hidden, precision=lax.Precision.HIGHEST, preferred_element_type=jnp.float32) + bias_out[:, None]
        optical = jax.nn.softplus(raw_out[0]) * occupied * step_size
        contrib = contrib + jnp.exp(-depth_sum) * (1.0 - jnp.exp(-optical)) * raw_out[1:]
        return (contrib, depth_sum + optical), None

    start = (jnp.zeros((FEAT, ray_count), jnp.float32), jnp.zeros((ray_count,), jnp.float32))
    (contrib, depth_sum), unused = lax.scan(sample_step, start, jnp.arange(total_samples, dtype=jnp.int32))
    stored = contrib.reshape(FEAT, image_cols, N_ROW, HB)
    band_index = jnp.arange(N_ROW, dtype=jnp.int32)[:, None] + jnp.zeros((1, HB), jnp.int32)
    inverse = jnp.zeros((N_ROW, HB), jnp.int32).at[band_index, ray_order].set(band_index * 0 + jnp.arange(HB, dtype=jnp.int32)[None, :])
    image = jnp.take_along_axis(stored, inverse[None, None], axis=3).reshape(FEAT, image_cols, image_rows)
    first = jax.nn.relu(convolve(image, kernel_first, bias_first))
    return convolve(first, kernel_second, bias_second)
```

```python
import functools

import jax
import jax.numpy as jnp
from jax import lax
from jax.experimental import pallas as pl
from jax.experimental.pallas import tpu as pltpu
from jax.sharding import PartitionSpec as P

MESH = pl.DeviceIdType.MESH
F32 = jnp.float32
BF16 = jnp.bfloat16
NT = (((1,), (1,)), ((), ()))
OFFSETS = [(dr, dc) for dr in (-1, 0, 1) for dc in (-1, 0, 1) if (dr, dc) != (0, 0)]


def split(x):
    hi = x.astype(BF16)
    lo = (x - hi.astype(F32)).astype(BF16)
    return hi, lo


def dot(a, b):
    return jnp.dot(a, b, preferred_element_type=F32)


def dot_nt(a, b):
    return lax.dot_general(a, b, NT, preferred_element_type=F32)


def kernel(
    sizes,
    vox,
    counts,
    order,
    w_in,
    b_in,
    w_out,
    b_out,
    k1,
    b1,
    k2,
    b2,
    out,
    send,
    recv,
    raw_buf,
    dens,
    own,
    side,
    edge,
    pad,
    firsts,
    base1,
    base2,
    wide,
    t1h,
    t1l,
    t2h,
    t2l,
    a2a_send,
    a2a_recv,
    halo_send,
    halo_recv,
):
    n_depth, n_row, n_col, slots, chans, step_size = sizes
    cw = 4
    depth = lax.axis_index("depth")
    row = lax.axis_index("row")
    col = lax.axis_index("col")
    tile = depth * n_col + col
    tiles = n_depth * n_col

    def exists(dr, dc):
        r, t = row + dr, tile + dc
        return (r >= 0) & (r < n_row) & (t >= 0) & (t < tiles)

    def device(dr, dc):
        t = tile + dc
        return {"depth": t // n_col, "row": row + dr, "col": t % n_col}

    barrier = pltpu.get_barrier_semaphore()

    def greet(i, carry):
        pl.semaphore_signal(
            barrier,
            inc=1,
            device_id={"depth": (depth + 1 + i) % n_depth},
            device_id_type=MESH,
        )
        return carry

    lax.fori_loop(0, n_depth - 1, greet, 0)
    arrivals = jnp.int32(n_depth - 1)
    for dr, dc in OFFSETS:
        there = exists(dr, dc)
        arrivals = arrivals + there.astype(jnp.int32)

        @pl.when(there)
        def _():
            pl.semaphore_signal(
                barrier, inc=1, device_id=device(dr, dc), device_id_type=MESH
            )

    wi = w_in[...]
    wi_hi = wi.astype(BF16).astype(F32)
    wi_lo = wi - wi_hi
    bi = b_in[...]
    bi_hi = bi.astype(BF16).astype(F32)
    bi_mid = (bi - bi_hi).astype(BF16).astype(F32)
    bi_lo = bi - bi_hi - bi_mid
    rows8 = lax.broadcasted_iota(jnp.int32, (8, 128), 0)
    bias_rows = jnp.where(
        rows8 == 0, bi_hi, jnp.where(rows8 == 1, bi_mid, jnp.where(rows8 == 2, bi_lo, 0.0))
    )
    stacked = jnp.concatenate(
        [wi_hi, wi_hi, wi_lo, bias_rows, jnp.zeros((96, 128), F32)], axis=0
    )
    lhs1 = stacked.T[:, :32].astype(BF16)
    wide[...] = jnp.zeros((128, 128), F32)
    wide[:, 0:33] = w_out[...]
    wt = pltpu.roll(wide[...], 127, 1).T
    w40 = jnp.concatenate([wt[0:32], wt[120:128]], axis=0)
    w40_hi = w40.astype(BF16).astype(F32)
    w40_lo = w40 - w40_hi
    lhs2 = jnp.concatenate(
        [
            jnp.concatenate([w40_hi, w40_hi], axis=1),
            jnp.concatenate([w40_lo, jnp.zeros_like(w40_lo)], axis=1),
        ],
        axis=0,
    ).astype(BF16)
    wide[0:8, :] = jnp.zeros((8, 128), F32)
    wide[0:1, 0:33] = b_out[...]
    bo = pltpu.roll(jnp.broadcast_to(wide[0:1, :], (128, 128)), 127, 1).T
    bo_feat = jnp.concatenate([bo[0:32]] * cw, axis=1)
    bo_dens = jnp.concatenate([bo[127:128]] * cw, axis=1)

    lanes = cw * 128
    ones8 = jnp.ones((8, lanes), F32)
    slot_iota = lax.broadcasted_iota(jnp.int32, (8, lanes), 0)

    def a2a_copy(peer, slot, sem):
        return pltpu.make_async_remote_copy(
            src_ref=send.at[peer],
            dst_ref=recv.at[slot],
            send_sem=a2a_send.at[peer],
            recv_sem=a2a_recv.at[sem],
            device_id={"depth": peer},
            device_id_type=MESH,
        )

    def block_step(i, carry):
        block = (depth + 1 + i) % n_depth
        for s in range(slots):
            x = jnp.concatenate(
                [
                    vox[
                        pl.ds(
                            s * (chans * n_depth * cw) + block * cw + w,
                            chans,
                            stride=n_depth * cw,
                        ),
                        :,
                    ]
                    for w in range(cw)
                ],
                axis=1,
            )
            x_hi = x.astype(BF16).astype(F32)
            rhs1 = jnp.concatenate([x_hi, x - x_hi, x_hi, ones8], axis=0).astype(BF16)
            hidden = jnp.maximum(dot(lhs1, rhs1), 0.0)
            h_hi, h_lo = split(hidden)
            r = dot(lhs2, jnp.concatenate([h_hi, h_lo], axis=0))
            raw = r[0:40] + r[40:80]
            raw_buf[s] = raw[0:32]
            dens[s : s + 1, :] = raw[39:40]
        cnt = jnp.concatenate(
            [counts[pl.ds(block * cw + w, 1), :] for w in range(cw)], axis=1
        )
        raw0 = dens[...] + bo_dens
        soft = jnp.maximum(raw0, 0.0) + jnp.log1p(jnp.exp(-jnp.abs(raw0)))
        tau = jnp.where(slot_iota < cnt, soft * step_size, 0.0)
        inc = tau
        for shift in (1, 2, 4):
            inc = inc + jnp.where(slot_iota >= shift, pltpu.roll(inc, shift, 0), 0.0)
        after = jnp.exp(-inc)
        before = jnp.where(slot_iota == 0, 1.0, pltpu.roll(after, 1, 0))
        weight = before - after
        contrib = bo_feat * (1.0 - after[7:8])
        for s in range(slots):
            contrib = contrib + weight[s : s + 1] * raw_buf[s]
        for w in range(cw):
            send[block, w * 32 : (w + 1) * 32, :] = contrib[:, w * 128 : (w + 1) * 128]
        for w in range(cw):
            send[block, 128 + w : 129 + w, :] = inc[7:8, w * 128 : (w + 1) * 128]

        @pl.when(i == 0)
        def _():
            pl.semaphore_wait(barrier, arrivals)

        @pl.when(i < n_depth - 1)
        def _():
            a2a_copy(block, depth, depth).start()

        return carry

    lax.fori_loop(0, n_depth, block_step, 0)
    recv[depth] = send[depth]

    base1[...] = jnp.zeros(base1.shape, F32)
    base2[...] = jnp.zeros(base2.shape, F32)
    for b in range(3):
        for a in range(3):
            at = (a * 3 + b) * 64
            base1[:, a * 32 : (a + 1) * 32] = k1[at : at + 64, :]
            base2[:, a * 64 : (a + 1) * 64] = k2[at : at + 64, :]
        block1 = base1[...]
        for place, w in enumerate((0, 1, 2, 3, 4, -1)):
            shift = (32 * (w - 1)) % 256
            hi, lo = split(pltpu.roll(block1, shift, 1) if shift else block1)
            t1h[b, place * 64 : (place + 1) * 64, :] = hi
            t1l[b, place * 64 : (place + 1) * 64, :] = lo
        block2 = base2[...]
        for w in range(4):
            shift = (64 * (w - 1)) % 384
            hi, lo = split(pltpu.roll(block2, shift, 1) if shift else block2)
            t2h[b, w * 64 : (w + 1) * 64, :] = hi
            t2l[b, w * 64 : (w + 1) * 64, :] = lo
    bias1 = jnp.concatenate([b1[...]] * 6, axis=1)
    wide[0:1, 0:64] = b2[...]
    bias2 = jnp.broadcast_to(wide[0:1, :], (128, 128)).T[0:64]
    select = (
        lax.broadcasted_iota(jnp.int32, (128, 128), 0) == order[...]
    ).astype(F32).astype(BF16)

    for i, (dr, dc) in enumerate(OFFSETS):
        slot = side.at[(dc + 1) // 2] if dr == 0 else edge.at[(dr + 1) // 2, dc + 1]

        @pl.when(jnp.logical_not(exists(dr, dc)))
        def _():
            slot[...] = jnp.zeros(slot.shape, F32)

    def gather(k, carry):
        before, parts = carry

        @pl.when(k != depth)
        def _():
            a2a_copy(k, k, k).wait_recv()

        fade = jnp.exp(-before)
        parts = tuple(
            parts[w] + fade[w : w + 1] * recv[k, w * 32 : (w + 1) * 32, :]
            for w in range(cw)
        )
        return before + recv[k, 128:136, :], parts

    zero = jnp.zeros((32, 128), F32)
    before, parts = lax.fori_loop(
        0, n_depth, gather, (jnp.zeros((8, 128), F32), (zero,) * cw)
    )
    c_hi, c_lo = split(jnp.concatenate(parts, axis=0))
    image = dot_nt(
        jnp.concatenate([select, select], axis=1), jnp.concatenate([c_hi, c_lo], axis=1)
    )
    own[...] = image

    def halo_copy(i, dr, dc, target=None):
        back = OFFSETS.index((-dr, -dc))
        if dr == 0:
            src, dst = own, side.at[(1 - dc) // 2]
        else:
            src = own.at[0:8] if dr < 0 else own.at[120:128]
            dst = edge.at[(1 - dr) // 2, 1 - dc]
        return pltpu.make_async_remote_copy(
            src_ref=src,
            dst_ref=dst,
            send_sem=halo_send.at[i],
            recv_sem=halo_recv.at[back],
            device_id=device(dr, dc) if target is None else target,
            device_id_type=MESH,
        )

    for i, (dr, dc) in enumerate(OFFSETS):

        @pl.when(exists(dr, dc))
        def _():
            halo_copy(i, dr, dc).start()

    def drain(i, carry):
        a2a_copy((depth + 1 + i) % n_depth, depth, depth).wait_send()
        return carry

    lax.fori_loop(0, n_depth - 1, drain, 0)

    for i, (dr, dc) in enumerate(OFFSETS):

        @pl.when(exists(dr, dc))
        def _():
            j = OFFSETS.index((-dr, -dc))
            halo_copy(j, -dr, -dc, device(dr, dc)).wait_recv()

    lane = lax.broadcasted_iota(jnp.int32, (128, 128), 1)
    pad[8:136, 0:128] = image
    pad[8:136, 128:256] = jnp.where(lane < 64, side[1], side[0])
    pad[0:8, 0:128] = edge[0, 1]
    pad[0:8, 128:256] = jnp.where(lane[0:8] < 64, edge[0, 2], edge[0, 0])
    pad[136:144, 0:128] = edge[1, 1]
    pad[136:144, 128:256] = jnp.where(lane[0:8] < 64, edge[1, 2], edge[1, 0])
    pad[144:152, :] = jnp.zeros((8, 256), F32)

    total = jnp.zeros((144, 384), F32) + bias1
    for b in range(3):
        hi, lo = split(pad[6 + b : 150 + b, :])
        total = total + dot_nt(hi, t1h[b]) + dot_nt(lo, t1h[b]) + dot_nt(hi, t1l[b])
    h = lax.broadcasted_iota(jnp.int32, (144, 384), 0)
    place = lax.broadcasted_iota(jnp.int32, (144, 384), 1) // 64
    outside = (
        ((h == 0) & (row == 0))
        | ((h == 129) & (row == n_row - 1))
        | ((place == 5) & (tile == 0))
        | ((place == 4) & (tile == tiles - 1))
    )
    firsts[...] = jnp.where(outside, 0.0, jnp.maximum(total, 0.0))

    final = jnp.concatenate([bias2] * 4, axis=0)
    for b in range(3):
        hi, lo = split(firsts[b : 128 + b, :])
        final = final + dot_nt(t2h[b], hi) + dot_nt(t2h[b], lo) + dot_nt(t2l[b], hi)
    for w in range(4):
        out[pl.ds(w, 64, stride=4), :] = final[w * 64 : (w + 1) * 64]

    for i, (dr, dc) in enumerate(OFFSETS):

        @pl.when(exists(dr, dc))
        def _():
            halo_copy(i, dr, dc).wait_send()


def on_device(
    voxels,
    counts,
    ray_order,
    weight_in,
    bias_in,
    weight_out,
    bias_out,
    kernel_first,
    bias_first,
    kernel_second,
    bias_second,
):
    slots, chans, n_depth, cw, hb = voxels.shape
    n_row = lax.axis_size("row")
    n_col = lax.axis_size("col")
    step_size = 2.0 / (slots * n_depth)
    out_ch = kernel_second.shape[2]
    sizes = (n_depth, n_row, n_col, slots, chans, step_size)
    vmem = pl.BlockSpec(memory_space=pltpu.VMEM)
    out = pl.pallas_call(
        functools.partial(kernel, sizes),
        out_shape=jax.ShapeDtypeStruct((out_ch * cw, hb), F32),
        in_specs=[vmem] * 11,
        out_specs=vmem,
        scratch_shapes=[
            pltpu.VMEM((n_depth, 136, 128), F32),
            pltpu.VMEM((n_depth, 136, 128), F32),
            pltpu.VMEM((slots, 32, 512), F32),
            pltpu.VMEM((8, 512), F32),
            pltpu.VMEM((128, 128), F32),
            pltpu.VMEM((2, 128, 128), F32),
            pltpu.VMEM((2, 3, 8, 128), F32),
            pltpu.VMEM((152, 256), F32),
            pltpu.VMEM((144, 384), F32),
            pltpu.VMEM((64, 256), F32),
            pltpu.VMEM((64, 384), F32),
            pltpu.VMEM((128, 128), F32),
            pltpu.VMEM((3, 384, 256), BF16),
            pltpu.VMEM((3, 384, 256), BF16),
            pltpu.VMEM((3, 256, 384), BF16),
            pltpu.VMEM((3, 256, 384), BF16),
            pltpu.SemaphoreType.DMA((n_depth,)),
            pltpu.SemaphoreType.DMA((n_depth,)),
            pltpu.SemaphoreType.DMA((8,)),
            pltpu.SemaphoreType.DMA((8,)),
        ],
        compiler_params=pltpu.CompilerParams(
            collective_id=0,
            has_side_effects=True,
            vmem_limit_bytes=40 * 1024 * 1024,
        ),
    )(
        voxels.reshape(slots * chans * n_depth * cw, hb),
        counts.reshape(n_depth * cw, hb),
        ray_order,
        weight_in,
        bias_in.reshape(1, -1),
        weight_out,
        bias_out.reshape(1, -1),
        kernel_first.reshape(-1, kernel_first.shape[3]),
        bias_first.reshape(1, -1),
        kernel_second.reshape(-1, kernel_second.shape[3]),
        bias_second.reshape(1, -1),
    )
    return out.reshape(out_ch, cw, hb)


def solution(mesh):
    in_specs = (
        P("depth", None, None, "col", ("groups", "row")),
        P("depth", None, "col", ("groups", "row")),
        P(("groups", "row"), None),
        P(),
        P(),
        P(),
        P(),
        P(),
        P(),
        P(),
        P(),
    )
    out_specs = P(None, ("depth", "col"), ("groups", "row"))
    return jax.shard_map(
        on_device, mesh=mesh, in_specs=in_specs, out_specs=out_specs, check_vma=False
    )
```

```python
import functools

import jax
import jax.numpy as jnp
from jax import lax
from jax.experimental import pallas as pl
from jax.experimental.pallas import tpu as pltpu
from jax.sharding import PartitionSpec as P

MESH = pl.DeviceIdType.MESH
F32 = jnp.float32
BF16 = jnp.bfloat16
NT = (((1,), (1,)), ((), ()))
OFFSETS = [(dr, dc) for dr in (-1, 0, 1) for dc in (-1, 0, 1) if (dr, dc) != (0, 0)]


def split(x):
    hi = x.astype(BF16)
    lo = (x - hi.astype(F32)).astype(BF16)
    return hi, lo


def dot(a, b):
    return jnp.dot(a, b, preferred_element_type=F32)


def dot_nt(a, b):
    return lax.dot_general(a, b, NT, preferred_element_type=F32)


def kernel(
    sizes,
    *refs,
):
    operands, out, held = refs[:11], refs[11], refs[12:23]
    (
    send,
    recv,
    raw_buf,
    dens,
    own,
    side,
    edge,
    pad,
    firsts,
    wide,
    t1h,
    t1l,
    t2h,
    t2l,
    a2a_send,
    a2a_recv,
    halo_send,
    halo_recv,
    load_sem,
    ) = refs[23:]
    vox, counts, order, w_in, b_in, w_out, b_out, k1, b1, k2, b2 = held
    loads = [
        pltpu.make_async_copy(src, dst, load_sem.at[i])
        for i, (src, dst) in enumerate(zip(operands, held))
    ]
    for i in (3, 4, 5, 6, 0, 1, 2, 7, 8, 9, 10):
        loads[i].start()
    n_depth, n_row, n_col, slots, chans, step_size = sizes
    cw = 4
    depth = lax.axis_index("depth")
    row = lax.axis_index("row")
    col = lax.axis_index("col")
    tile = depth * n_col + col
    tiles = n_depth * n_col

    def exists(dr, dc):
        r, t = row + dr, tile + dc
        return (r >= 0) & (r < n_row) & (t >= 0) & (t < tiles)

    def device(dr, dc):
        t = tile + dc
        return {"depth": t // n_col, "row": row + dr, "col": t % n_col}

    barrier = pltpu.get_barrier_semaphore()

    def greet(i, carry):
        pl.semaphore_signal(
            barrier,
            inc=1,
            device_id={"depth": (depth + 1 + i) % n_depth},
            device_id_type=MESH,
        )
        return carry

    lax.fori_loop(0, n_depth - 1, greet, 0)
    arrivals = jnp.int32(n_depth - 1)
    for dr, dc in OFFSETS:
        there = exists(dr, dc)
        arrivals = arrivals + there.astype(jnp.int32)

        @pl.when(there)
        def _():
            pl.semaphore_signal(
                barrier, inc=1, device_id=device(dr, dc), device_id_type=MESH
            )

    for i in (3, 4, 5, 6):
        loads[i].wait()
    wi = w_in[...]
    wi_hi = wi.astype(BF16).astype(F32)
    wi_lo = wi - wi_hi
    bi = b_in[...]
    bi_hi = bi.astype(BF16).astype(F32)
    bi_mid = (bi - bi_hi).astype(BF16).astype(F32)
    bi_lo = bi - bi_hi - bi_mid
    rows8 = lax.broadcasted_iota(jnp.int32, (8, 128), 0)
    bias_rows = jnp.where(
        rows8 == 0, bi_hi, jnp.where(rows8 == 1, bi_mid, jnp.where(rows8 == 2, bi_lo, 0.0))
    )
    stacked = jnp.concatenate(
        [wi_hi, wi_hi, wi_lo, bias_rows, jnp.zeros((96, 128), F32)], axis=0
    )
    lhs1 = stacked.T[:, :32].astype(BF16)
    wide[0:32, :] = w_out[1:33, :]
    wide[32:40, :] = jnp.zeros((8, 128), F32)
    wide[39:40, :] = w_out[0:1, :]
    w40 = wide[0:40, :]
    w40_hi = w40.astype(BF16).astype(F32)
    w40_lo = w40 - w40_hi
    lhs2 = jnp.concatenate(
        [
            jnp.concatenate([w40_hi, w40_hi], axis=1),
            jnp.concatenate([w40_lo, jnp.zeros_like(w40_lo)], axis=1),
        ],
        axis=0,
    ).astype(BF16)
    wide[0:8, :] = jnp.zeros((8, 128), F32)
    wide[0:1, 0:33] = b_out[...]
    bo = pltpu.roll(jnp.broadcast_to(wide[0:1, :], (128, 128)), 127, 1).T
    bo_feat = jnp.concatenate([bo[0:32]] * cw, axis=1)
    bo_dens = jnp.concatenate([bo[127:128]] * cw, axis=1)

    for i in (0, 1):
        loads[i].wait()
    lanes = cw * 128
    ones8 = jnp.ones((8, lanes), F32)
    slot_iota = lax.broadcasted_iota(jnp.int32, (8, lanes), 0)

    def a2a_copy(peer, slot, sem):
        return pltpu.make_async_remote_copy(
            src_ref=send.at[peer],
            dst_ref=recv.at[slot],
            send_sem=a2a_send.at[peer],
            recv_sem=a2a_recv.at[sem],
            device_id={"depth": peer},
            device_id_type=MESH,
        )

    def block_step(i, carry):
        block = (depth + 1 + i) % n_depth
        for s in range(slots):
            x = jnp.concatenate(
                [
                    vox[
                        pl.ds(
                            s * (chans * n_depth * cw) + block * cw + w,
                            chans,
                            stride=n_depth * cw,
                        ),
                        :,
                    ]
                    for w in range(cw)
                ],
                axis=1,
            )
            x_hi = x.astype(BF16).astype(F32)
            rhs1 = jnp.concatenate([x_hi, x - x_hi, x_hi, ones8], axis=0).astype(BF16)
            hidden = jnp.maximum(dot(lhs1, rhs1), 0.0)
            h_hi, h_lo = split(hidden)
            r = dot(lhs2, jnp.concatenate([h_hi, h_lo], axis=0))
            raw = r[0:40] + r[40:80]
            raw_buf[s] = raw[0:32]
            dens[s : s + 1, :] = raw[39:40]
        cnt = jnp.concatenate(
            [counts[pl.ds(block * cw + w, 1), :] for w in range(cw)], axis=1
        )
        raw0 = dens[...] + bo_dens
        soft = jnp.maximum(raw0, 0.0) + jnp.log1p(jnp.exp(-jnp.abs(raw0)))
        tau = jnp.where(slot_iota < cnt, soft * step_size, 0.0)
        inc = tau
        for shift in (1, 2, 4):
            inc = inc + jnp.where(slot_iota >= shift, pltpu.roll(inc, shift, 0), 0.0)
        after = jnp.exp(-inc)
        before = jnp.where(slot_iota == 0, 1.0, pltpu.roll(after, 1, 0))
        weight = before - after
        contrib = bo_feat * (1.0 - after[7:8])
        for s in range(slots):
            contrib = contrib + weight[s : s + 1] * raw_buf[s]
        for w in range(cw):
            send[block, w * 32 : (w + 1) * 32, :] = contrib[:, w * 128 : (w + 1) * 128]
        for w in range(cw):
            send[block, 128 + w : 129 + w, :] = inc[7:8, w * 128 : (w + 1) * 128]

        @pl.when(i == 0)
        def _():
            pl.semaphore_wait(barrier, arrivals)

        @pl.when(i < n_depth - 1)
        def _():
            a2a_copy(block, depth, depth).start()

        return carry

    lax.fori_loop(0, n_depth, block_step, 0)
    recv[depth] = send[depth]

    for i in (2, 7, 8, 9, 10):
        loads[i].wait()
    left = lax.broadcasted_iota(jnp.int32, (64, 128), 1) < 64

    def halves(kernels, first, second):
        keep = left[0 : kernels[0].shape[0]]
        zeros = jnp.zeros(keep.shape, F32)
        return split(
            jnp.where(
                keep,
                kernels[first] if 0 <= first <= 2 else zeros,
                kernels[second] if 0 <= second <= 2 else zeros,
            )
        )

    pairs = ((0, 1), (2, 3), (4, -1))
    for b in range(3):
        firsts_k = []
        seconds_k = []
        for a in range(3):
            one = k1[(a * 3 + b) * 32 : (a * 3 + b + 1) * 32, :]
            two = k2[(a * 3 + b) * 64 : (a * 3 + b + 1) * 64, :]
            firsts_k.append(jnp.concatenate([one, one], axis=1))
            seconds_k.append(jnp.concatenate([two, two], axis=1))
        for p, (w0, w1) in enumerate(pairs):
            for position, x in enumerate((0, 1, 2, 3, 4, 5, -2, -1)):
                hi, lo = halves(firsts_k, x - w0 + 1, x - w1 + 1)
                at = (b, pl.ds(position * 32, 32), pl.ds(p * 128, 128))
                t1h[at] = hi
                t1l[at] = lo
            for w in range(4):
                hi, lo = halves(seconds_k, w0 - w + 1, w1 - w + 1)
                at = (b, pl.ds(w * 64, 64), pl.ds(p * 128, 128))
                t2h[at] = hi
                t2l[at] = lo
    bias1 = jnp.concatenate([b1[...]] * 6, axis=1)
    wide[0:1, 0:64] = b2[...]
    bias2 = jnp.broadcast_to(wide[0:1, :], (128, 128)).T[0:64]
    select = (
        lax.broadcasted_iota(jnp.int32, (128, 128), 0) == order[...]
    ).astype(F32).astype(BF16)

    for i, (dr, dc) in enumerate(OFFSETS):
        slot = side.at[(dc + 1) // 2] if dr == 0 else edge.at[(dr + 1) // 2, dc + 1]

        @pl.when(jnp.logical_not(exists(dr, dc)))
        def _():
            slot[...] = jnp.zeros(slot.shape, F32)

    def gather(k, carry):
        before, parts = carry

        @pl.when(k != depth)
        def _():
            a2a_copy(k, k, k).wait_recv()

        fade = jnp.exp(-before)
        parts = tuple(
            parts[w] + fade[w : w + 1] * recv[k, w * 32 : (w + 1) * 32, :]
            for w in range(cw)
        )
        return before + recv[k, 128:136, :], parts

    zero = jnp.zeros((32, 128), F32)
    before, parts = lax.fori_loop(
        0, n_depth, gather, (jnp.zeros((8, 128), F32), (zero,) * cw)
    )
    c_hi, c_lo = split(jnp.concatenate(parts, axis=0))
    image = dot_nt(
        jnp.concatenate([select, select], axis=1), jnp.concatenate([c_hi, c_lo], axis=1)
    )
    own[...] = image

    def halo_copy(i, dr, dc, target=None):
        back = OFFSETS.index((-dr, -dc))
        if dr == 0:
            src, dst = own, side.at[(1 - dc) // 2]
        else:
            src = own.at[0:8] if dr < 0 else own.at[120:128]
            dst = edge.at[(1 - dr) // 2, 1 - dc]
        return pltpu.make_async_remote_copy(
            src_ref=src,
            dst_ref=dst,
            send_sem=halo_send.at[i],
            recv_sem=halo_recv.at[back],
            device_id=device(dr, dc) if target is None else target,
            device_id_type=MESH,
        )

    for i, (dr, dc) in enumerate(OFFSETS):

        @pl.when(exists(dr, dc))
        def _():
            halo_copy(i, dr, dc).start()

    def drain(i, carry):
        a2a_copy((depth + 1 + i) % n_depth, depth, depth).wait_send()
        return carry

    lax.fori_loop(0, n_depth - 1, drain, 0)

    for i, (dr, dc) in enumerate(OFFSETS):

        @pl.when(exists(dr, dc))
        def _():
            j = OFFSETS.index((-dr, -dc))
            halo_copy(j, -dr, -dc, device(dr, dc)).wait_recv()

    lane = lax.broadcasted_iota(jnp.int32, (128, 128), 1)
    pad[8:136, 0:128] = image
    pad[8:136, 128:256] = jnp.where(lane < 64, side[1], side[0])
    pad[0:8, 0:128] = edge[0, 1]
    pad[0:8, 128:256] = jnp.where(lane[0:8] < 64, edge[0, 2], edge[0, 0])
    pad[136:144, 0:128] = edge[1, 1]
    pad[136:144, 128:256] = jnp.where(lane[0:8] < 64, edge[1, 2], edge[1, 0])
    pad[144:152, :] = jnp.zeros((8, 256), F32)

    total = jnp.zeros((144, 384), F32) + bias1
    for b in range(3):
        hi, lo = split(pad[6 + b : 150 + b, :])
        total = total + dot(hi, t1h[b]) + dot(lo, t1h[b]) + dot(hi, t1l[b])
    h = lax.broadcasted_iota(jnp.int32, (144, 384), 0)
    place = lax.broadcasted_iota(jnp.int32, (144, 384), 1) // 64
    outside = (
        ((h == 0) & (row == 0))
        | ((h == 129) & (row == n_row - 1))
        | ((place == 5) & (tile == 0))
        | ((place == 4) & (tile == tiles - 1))
    )
    firsts[...] = jnp.where(outside, 0.0, jnp.maximum(total, 0.0))

    final = jnp.concatenate([bias2] * 4, axis=0)
    for b in range(3):
        hi, lo = split(firsts[b : 128 + b, :])
        final = final + dot_nt(t2h[b], hi) + dot_nt(t2h[b], lo) + dot_nt(t2l[b], hi)
    for w in range(4):
        out[pl.ds(w, 64, stride=4), :] = final[w * 64 : (w + 1) * 64]

    for i, (dr, dc) in enumerate(OFFSETS):

        @pl.when(exists(dr, dc))
        def _():
            halo_copy(i, dr, dc).wait_send()


def on_device(
    voxels,
    counts,
    ray_order,
    weight_in,
    bias_in,
    weight_out,
    bias_out,
    kernel_first,
    bias_first,
    kernel_second,
    bias_second,
):
    slots, chans, n_depth, cw, hb = voxels.shape
    n_row = lax.axis_size("row")
    n_col = lax.axis_size("col")
    step_size = 2.0 / (slots * n_depth)
    out_ch = kernel_second.shape[2]
    sizes = (n_depth, n_row, n_col, slots, chans, step_size)
    vmem = pl.BlockSpec(memory_space=pltpu.VMEM)
    operands = (
        voxels.reshape(slots * chans * n_depth * cw, hb),
        counts.reshape(n_depth * cw, hb),
        ray_order,
        weight_in,
        bias_in.reshape(1, -1),
        weight_out.T,
        bias_out.reshape(1, -1),
        kernel_first.transpose(0, 1, 3, 2).reshape(-1, kernel_first.shape[2]),
        bias_first.reshape(1, -1),
        kernel_second.reshape(-1, kernel_second.shape[3]),
        bias_second.reshape(1, -1),
    )
    out = pl.pallas_call(
        functools.partial(kernel, sizes),
        out_shape=jax.ShapeDtypeStruct((out_ch * cw, hb), F32),
        in_specs=[pl.BlockSpec(memory_space=pltpu.HBM)] * 11,
        out_specs=vmem,
        scratch_shapes=[pltpu.VMEM(x.shape, x.dtype) for x in operands]
        + [
            pltpu.VMEM((n_depth, 136, 128), F32),
            pltpu.VMEM((n_depth, 136, 128), F32),
            pltpu.VMEM((slots, 32, 512), F32),
            pltpu.VMEM((8, 512), F32),
            pltpu.VMEM((128, 128), F32),
            pltpu.VMEM((2, 128, 128), F32),
            pltpu.VMEM((2, 3, 8, 128), F32),
            pltpu.VMEM((152, 256), F32),
            pltpu.VMEM((144, 384), F32),
            pltpu.VMEM((128, 128), F32),
            pltpu.VMEM((3, 256, 384), BF16),
            pltpu.VMEM((3, 256, 384), BF16),
            pltpu.VMEM((3, 256, 384), BF16),
            pltpu.VMEM((3, 256, 384), BF16),
            pltpu.SemaphoreType.DMA((n_depth,)),
            pltpu.SemaphoreType.DMA((n_depth,)),
            pltpu.SemaphoreType.DMA((8,)),
            pltpu.SemaphoreType.DMA((8,)),
            pltpu.SemaphoreType.DMA((11,)),
        ],
        compiler_params=pltpu.CompilerParams(
            collective_id=0,
            has_side_effects=True,
            vmem_limit_bytes=64000 * 1024,
        ),
    )(*operands)
    return out.reshape(out_ch, cw, hb)


def solution(mesh):
    in_specs = (
        P("depth", None, None, "col", ("groups", "row")),
        P("depth", None, "col", ("groups", "row")),
        P(("groups", "row"), None),
        P(),
        P(),
        P(),
        P(),
        P(),
        P(),
        P(),
        P(),
    )
    out_specs = P(None, ("depth", "col"), ("groups", "row"))
    return jax.shard_map(
        on_device, mesh=mesh, in_specs=in_specs, out_specs=out_specs, check_vma=False
    )
```

```python
import functools

import jax
import jax.numpy as jnp
from jax import lax
from jax.experimental import pallas as pl
from jax.experimental.pallas import tpu as pltpu
from jax.sharding import PartitionSpec as P

MESH = pl.DeviceIdType.MESH
F32 = jnp.float32
BF16 = jnp.bfloat16
NT = (((1,), (1,)), ((), ()))
OFFSETS = [(dr, dc) for dr in (-1, 0, 1) for dc in (-1, 0, 1) if (dr, dc) != (0, 0)]


def split(x):
    hi = x.astype(BF16)
    lo = (x - hi.astype(F32)).astype(BF16)
    return hi, lo


def dot(a, b):
    return jnp.dot(a, b, preferred_element_type=F32)


def dot_nt(a, b):
    return lax.dot_general(a, b, NT, preferred_element_type=F32)


def kernel(
    sizes,
    *refs,
):
    operands, out, held = refs[:11], refs[11], refs[12:23]
    (
    send,
    recv,
    raw_buf,
    dens,
    own,
    side,
    edge,
    pad,
    firsts,
    wide,
    t1h,
    t1l,
    t2h,
    t2l,
    a2a_send,
    a2a_recv,
    halo_send,
    halo_recv,
    load_sem,
    ) = refs[23:]
    vox, counts, order, w_in, b_in, w_out, b_out, k1, b1, k2, b2 = held
    loads = [
        pltpu.make_async_copy(src, dst, load_sem.at[i])
        for i, (src, dst) in enumerate(zip(operands, held))
    ]
    for i in (3, 4, 5, 6, 0, 1, 2, 7, 8, 9, 10):
        loads[i].start()
    n_depth, n_row, n_col, slots, chans, step_size = sizes
    cw = 4
    depth = lax.axis_index("depth")
    row = lax.axis_index("row")
    col = lax.axis_index("col")
    tile = depth * n_col + col
    tiles = n_depth * n_col

    def exists(dr, dc):
        r, t = row + dr, tile + dc
        return (r >= 0) & (r < n_row) & (t >= 0) & (t < tiles)

    def device(dr, dc):
        t = tile + dc
        return {"depth": t // n_col, "row": row + dr, "col": t % n_col}

    barrier = pltpu.get_barrier_semaphore()

    def greet(i, carry):
        pl.semaphore_signal(
            barrier,
            inc=1,
            device_id={"depth": (depth + 1 + i) % n_depth},
            device_id_type=MESH,
        )
        return carry

    lax.fori_loop(0, n_depth - 1, greet, 0)
    arrivals = jnp.int32(n_depth - 1)
    for dr, dc in OFFSETS:
        there = exists(dr, dc)
        arrivals = arrivals + there.astype(jnp.int32)

        @pl.when(there)
        def _():
            pl.semaphore_signal(
                barrier, inc=1, device_id=device(dr, dc), device_id_type=MESH
            )

    for i in (3, 4, 5, 6):
        loads[i].wait()
    wi = w_in[...]
    wi_hi = wi.astype(BF16).astype(F32)
    wi_lo = wi - wi_hi
    bi = b_in[...]
    bi_hi = bi.astype(BF16).astype(F32)
    bi_mid = (bi - bi_hi).astype(BF16).astype(F32)
    bi_lo = bi - bi_hi - bi_mid
    rows8 = lax.broadcasted_iota(jnp.int32, (8, 128), 0)
    bias_rows = jnp.where(
        rows8 == 0, bi_hi, jnp.where(rows8 == 1, bi_mid, jnp.where(rows8 == 2, bi_lo, 0.0))
    )
    stacked = jnp.concatenate(
        [wi_hi, wi_hi, wi_lo, bias_rows, jnp.zeros((96, 128), F32)], axis=0
    )
    lhs1 = stacked.T[:, :32].astype(BF16)
    wide[0:32, :] = w_out[1:33, :]
    wide[32:40, :] = jnp.zeros((8, 128), F32)
    wide[39:40, :] = w_out[0:1, :]
    w40 = wide[0:40, :]
    w40_hi = w40.astype(BF16).astype(F32)
    w40_lo = w40 - w40_hi
    lhs2 = jnp.concatenate(
        [
            jnp.concatenate([w40_hi, w40_hi], axis=1),
            jnp.concatenate([w40_lo, jnp.zeros_like(w40_lo)], axis=1),
        ],
        axis=0,
    ).astype(BF16)
    wide[0:8, :] = jnp.zeros((8, 128), F32)
    wide[0:1, 0:33] = b_out[...]
    bo = pltpu.roll(jnp.broadcast_to(wide[0:1, :], (128, 128)), 127, 1).T
    bo_feat = jnp.concatenate([bo[0:32]] * cw, axis=1)
    bo_dens = jnp.concatenate([bo[127:128]] * cw, axis=1)

    for i in (0, 1):
        loads[i].wait()
    lanes = cw * 128
    ones8 = jnp.ones((8, lanes), F32)
    slot_iota = lax.broadcasted_iota(jnp.int32, (8, lanes), 0)

    def a2a_copy(peer, slot, sem):
        return pltpu.make_async_remote_copy(
            src_ref=send.at[peer],
            dst_ref=recv.at[slot],
            send_sem=a2a_send.at[peer],
            recv_sem=a2a_recv.at[sem],
            device_id={"depth": peer},
            device_id_type=MESH,
        )

    above = n_depth - 1 - depth

    def block_at(i):
        low = jnp.where(i < above, n_depth - 1 - i, i - above)
        high = jnp.where(i < depth, i, n_depth - 1 - i + depth)
        return jnp.where(depth * 2 < n_depth, low, high)

    def block_step(i, carry):
        block = block_at(i)
        for s in range(slots):
            x = jnp.concatenate(
                [
                    vox[
                        pl.ds(
                            s * (chans * n_depth * cw) + block * cw + w,
                            chans,
                            stride=n_depth * cw,
                        ),
                        :,
                    ]
                    for w in range(cw)
                ],
                axis=1,
            )
            x_hi = x.astype(BF16).astype(F32)
            rhs1 = jnp.concatenate([x_hi, x - x_hi, x_hi, ones8], axis=0).astype(BF16)
            hidden = jnp.maximum(dot(lhs1, rhs1), 0.0)
            h_hi, h_lo = split(hidden)
            r = dot(lhs2, jnp.concatenate([h_hi, h_lo], axis=0))
            raw = r[0:40] + r[40:80]
            raw_buf[s] = raw[0:32]
            dens[s : s + 1, :] = raw[39:40]
        cnt = jnp.concatenate(
            [counts[pl.ds(block * cw + w, 1), :] for w in range(cw)], axis=1
        )
        raw0 = dens[...] + bo_dens
        soft = jnp.maximum(raw0, 0.0) + jnp.log1p(jnp.exp(-jnp.abs(raw0)))
        tau = jnp.where(slot_iota < cnt, soft * step_size, 0.0)
        inc = tau
        for shift in (1, 2, 4):
            inc = inc + jnp.where(slot_iota >= shift, pltpu.roll(inc, shift, 0), 0.0)
        after = jnp.exp(-inc)
        before = jnp.where(slot_iota == 0, 1.0, pltpu.roll(after, 1, 0))
        weight = before - after
        contrib = bo_feat * (1.0 - after[7:8])
        for s in range(slots):
            contrib = contrib + weight[s : s + 1] * raw_buf[s]
        for w in range(cw):
            send[block, w * 32 : (w + 1) * 32, :] = contrib[:, w * 128 : (w + 1) * 128]
        for w in range(cw):
            send[block, 128 + w : 129 + w, :] = inc[7:8, w * 128 : (w + 1) * 128]

        @pl.when(i == 0)
        def _():
            pl.semaphore_wait(barrier, arrivals)

        @pl.when(i < n_depth - 1)
        def _():
            a2a_copy(block, depth, depth).start()

        return carry

    lax.fori_loop(0, n_depth, block_step, 0)
    recv[depth] = send[depth]

    for i in (2, 7, 8, 9, 10):
        loads[i].wait()
    left = lax.broadcasted_iota(jnp.int32, (64, 128), 1) < 64

    def halves(kernels, first, second):
        keep = left[0 : kernels[0].shape[0]]
        zeros = jnp.zeros(keep.shape, F32)
        return split(
            jnp.where(
                keep,
                kernels[first] if 0 <= first <= 2 else zeros,
                kernels[second] if 0 <= second <= 2 else zeros,
            )
        )

    pairs = ((0, 1), (2, 3), (4, -1))
    for b in range(3):
        firsts_k = []
        seconds_k = []
        for a in range(3):
            one = k1[(a * 3 + b) * 32 : (a * 3 + b + 1) * 32, :]
            two = k2[(a * 3 + b) * 64 : (a * 3 + b + 1) * 64, :]
            firsts_k.append(jnp.concatenate([one, one], axis=1))
            seconds_k.append(jnp.concatenate([two, two], axis=1))
        for p, (w0, w1) in enumerate(pairs):
            for position, x in enumerate((0, 1, 2, 3, 4, 5, -2, -1)):
                hi, lo = halves(firsts_k, x - w0 + 1, x - w1 + 1)
                at = (b, pl.ds(position * 32, 32), pl.ds(p * 128, 128))
                t1h[at] = hi
                t1l[at] = lo
            for w in range(4):
                hi, lo = halves(seconds_k, w0 - w + 1, w1 - w + 1)
                at = (b, pl.ds(w * 64, 64), pl.ds(p * 128, 128))
                t2h[at] = hi
                t2l[at] = lo
    bias1 = jnp.concatenate([b1[...]] * 6, axis=1)
    wide[0:1, 0:64] = b2[...]
    bias2 = jnp.broadcast_to(wide[0:1, :], (128, 128)).T[0:64]
    select = (
        lax.broadcasted_iota(jnp.int32, (128, 128), 0) == order[...]
    ).astype(F32).astype(BF16)

    for i, (dr, dc) in enumerate(OFFSETS):
        slot = side.at[(dc + 1) // 2] if dr == 0 else edge.at[(dr + 1) // 2, dc + 1]

        @pl.when(jnp.logical_not(exists(dr, dc)))
        def _():
            slot[...] = jnp.zeros(slot.shape, F32)

    def gather(k, carry):
        before, parts = carry

        @pl.when(k != depth)
        def _():
            a2a_copy(k, k, k).wait_recv()

        fade = jnp.exp(-before)
        parts = tuple(
            parts[w] + fade[w : w + 1] * recv[k, w * 32 : (w + 1) * 32, :]
            for w in range(cw)
        )
        return before + recv[k, 128:136, :], parts

    zero = jnp.zeros((32, 128), F32)
    before, parts = lax.fori_loop(
        0, n_depth, gather, (jnp.zeros((8, 128), F32), (zero,) * cw)
    )
    c_hi, c_lo = split(jnp.concatenate(parts, axis=0))
    image = dot_nt(
        jnp.concatenate([select, select], axis=1), jnp.concatenate([c_hi, c_lo], axis=1)
    )
    own[...] = image

    def halo_copy(i, dr, dc, target=None):
        back = OFFSETS.index((-dr, -dc))
        if dr == 0:
            src, dst = own, side.at[(1 - dc) // 2]
        else:
            src = own.at[0:8] if dr < 0 else own.at[120:128]
            dst = edge.at[(1 - dr) // 2, 1 - dc]
        return pltpu.make_async_remote_copy(
            src_ref=src,
            dst_ref=dst,
            send_sem=halo_send.at[i],
            recv_sem=halo_recv.at[back],
            device_id=device(dr, dc) if target is None else target,
            device_id_type=MESH,
        )

    for i, (dr, dc) in enumerate(OFFSETS):

        @pl.when(exists(dr, dc))
        def _():
            halo_copy(i, dr, dc).start()

    def drain(i, carry):
        a2a_copy((depth + 1 + i) % n_depth, depth, depth).wait_send()
        return carry

    lax.fori_loop(0, n_depth - 1, drain, 0)

    for i, (dr, dc) in enumerate(OFFSETS):

        @pl.when(exists(dr, dc))
        def _():
            j = OFFSETS.index((-dr, -dc))
            halo_copy(j, -dr, -dc, device(dr, dc)).wait_recv()

    lane = lax.broadcasted_iota(jnp.int32, (128, 128), 1)
    pad[8:136, 0:128] = image
    pad[8:136, 128:256] = jnp.where(lane < 64, side[1], side[0])
    pad[0:8, 0:128] = edge[0, 1]
    pad[0:8, 128:256] = jnp.where(lane[0:8] < 64, edge[0, 2], edge[0, 0])
    pad[136:144, 0:128] = edge[1, 1]
    pad[136:144, 128:256] = jnp.where(lane[0:8] < 64, edge[1, 2], edge[1, 0])
    pad[144:152, :] = jnp.zeros((8, 256), F32)

    total = jnp.zeros((144, 384), F32) + bias1
    for b in range(3):
        hi, lo = split(pad[6 + b : 150 + b, :])
        total = total + dot(hi, t1h[b]) + dot(lo, t1h[b]) + dot(hi, t1l[b])
    h = lax.broadcasted_iota(jnp.int32, (144, 384), 0)
    place = lax.broadcasted_iota(jnp.int32, (144, 384), 1) // 64
    outside = (
        ((h == 0) & (row == 0))
        | ((h == 129) & (row == n_row - 1))
        | ((place == 5) & (tile == 0))
        | ((place == 4) & (tile == tiles - 1))
    )
    firsts[...] = jnp.where(outside, 0.0, jnp.maximum(total, 0.0))

    final = jnp.concatenate([bias2] * 4, axis=0)
    for b in range(3):
        hi, lo = split(firsts[b : 128 + b, :])
        final = final + dot_nt(t2h[b], hi) + dot_nt(t2h[b], lo) + dot_nt(t2l[b], hi)
    for w in range(4):
        out[pl.ds(w, 64, stride=4), :] = final[w * 64 : (w + 1) * 64]

    for i, (dr, dc) in enumerate(OFFSETS):

        @pl.when(exists(dr, dc))
        def _():
            halo_copy(i, dr, dc).wait_send()


def on_device(
    voxels,
    counts,
    ray_order,
    weight_in,
    bias_in,
    weight_out,
    bias_out,
    kernel_first,
    bias_first,
    kernel_second,
    bias_second,
):
    slots, chans, n_depth, cw, hb = voxels.shape
    n_row = lax.axis_size("row")
    n_col = lax.axis_size("col")
    step_size = 2.0 / (slots * n_depth)
    out_ch = kernel_second.shape[2]
    sizes = (n_depth, n_row, n_col, slots, chans, step_size)
    vmem = pl.BlockSpec(memory_space=pltpu.VMEM)
    operands = (
        voxels.reshape(slots * chans * n_depth * cw, hb),
        counts.reshape(n_depth * cw, hb),
        ray_order,
        weight_in,
        bias_in.reshape(1, -1),
        weight_out.T,
        bias_out.reshape(1, -1),
        kernel_first.transpose(0, 1, 3, 2).reshape(-1, kernel_first.shape[2]),
        bias_first.reshape(1, -1),
        kernel_second.reshape(-1, kernel_second.shape[3]),
        bias_second.reshape(1, -1),
    )
    out = pl.pallas_call(
        functools.partial(kernel, sizes),
        out_shape=pltpu.VMEM((out_ch * cw, hb), F32),
        in_specs=[pl.BlockSpec(memory_space=pltpu.HBM)] * 11,
        out_specs=vmem,
        scratch_shapes=[pltpu.VMEM(x.shape, x.dtype) for x in operands]
        + [
            pltpu.VMEM((n_depth, 136, 128), F32),
            pltpu.VMEM((n_depth, 136, 128), F32),
            pltpu.VMEM((slots, 32, 512), F32),
            pltpu.VMEM((8, 512), F32),
            pltpu.VMEM((128, 128), F32),
            pltpu.VMEM((2, 128, 128), F32),
            pltpu.VMEM((2, 3, 8, 128), F32),
            pltpu.VMEM((152, 256), F32),
            pltpu.VMEM((144, 384), F32),
            pltpu.VMEM((128, 128), F32),
            pltpu.VMEM((3, 256, 384), BF16),
            pltpu.VMEM((3, 256, 384), BF16),
            pltpu.VMEM((3, 256, 384), BF16),
            pltpu.VMEM((3, 256, 384), BF16),
            pltpu.SemaphoreType.DMA((n_depth,)),
            pltpu.SemaphoreType.DMA((n_depth,)),
            pltpu.SemaphoreType.DMA((8,)),
            pltpu.SemaphoreType.DMA((8,)),
            pltpu.SemaphoreType.DMA((11,)),
        ],
        compiler_params=pltpu.CompilerParams(
            collective_id=0,
            has_side_effects=True,
            vmem_limit_bytes=40000 * 1024,
        ),
    )(*[pltpu.with_memory_space_constraint(x, pltpu.HBM) for x in operands])
    return out.reshape(out_ch, cw, hb)


def solution(mesh):
    in_specs = (
        P("depth", None, None, "col", ("groups", "row")),
        P("depth", None, "col", ("groups", "row")),
        P(("groups", "row"), None),
        P(),
        P(),
        P(),
        P(),
        P(),
        P(),
        P(),
        P(),
    )
    out_specs = P(None, ("depth", "col"), ("groups", "row"))
    return jax.shard_map(
        on_device, mesh=mesh, in_specs=in_specs, out_specs=out_specs, check_vma=False
    )
```

```python
import functools

import jax
import jax.numpy as jnp
from jax import lax
from jax.experimental import pallas as pl
from jax.experimental.pallas import tpu as pltpu
from jax.sharding import PartitionSpec as P

MESH = pl.DeviceIdType.MESH
F32 = jnp.float32
BF16 = jnp.bfloat16
NT = (((1,), (1,)), ((), ()))
OFFSETS = [(dr, dc) for dr in (-1, 0, 1) for dc in (-1, 0, 1) if (dr, dc) != (0, 0)]


def split(x):
    hi = x.astype(BF16)
    lo = (x - hi.astype(F32)).astype(BF16)
    return hi, lo


def dot(a, b):
    return jnp.dot(a, b, preferred_element_type=F32)


def dot_nt(a, b):
    return lax.dot_general(a, b, NT, preferred_element_type=F32)


def kernel(
    sizes,
    *refs,
):
    operands, out, held = refs[:11], refs[11], refs[12:23]
    (
    send,
    recv,
    raw_buf,
    dens,
    own,
    side,
    edge,
    pad,
    firsts,
    wide,
    t1h,
    t1l,
    t2h,
    t2l,
    a2a_send,
    a2a_recv,
    halo_send,
    halo_recv,
    load_sem,
    ) = refs[23:]
    vox, counts, order, w_in, b_in, w_out, b_out, k1, b1, k2, b2 = held
    loads = [
        pltpu.make_async_copy(src, dst, load_sem.at[i])
        for i, (src, dst) in enumerate(zip(operands, held))
    ]
    for i in (3, 4, 5, 6, 0, 1, 2, 7, 8, 9, 10):
        loads[i].start()
    n_depth, n_row, n_col, slots, chans, step_size = sizes
    cw = 4
    depth = lax.axis_index("depth")
    row = lax.axis_index("row")
    col = lax.axis_index("col")
    tile = depth * n_col + col
    tiles = n_depth * n_col

    def exists(dr, dc):
        r, t = row + dr, tile + dc
        return (r >= 0) & (r < n_row) & (t >= 0) & (t < tiles)

    def device(dr, dc):
        t = tile + dc
        return {"depth": t // n_col, "row": row + dr, "col": t % n_col}

    barrier = pltpu.get_barrier_semaphore()

    def greet(i, carry):
        pl.semaphore_signal(
            barrier,
            inc=1,
            device_id={"depth": (depth + 1 + i) % n_depth},
            device_id_type=MESH,
        )
        return carry

    lax.fori_loop(0, n_depth - 1, greet, 0)
    arrivals = jnp.int32(n_depth - 1)
    for dr, dc in OFFSETS:
        there = exists(dr, dc)
        arrivals = arrivals + there.astype(jnp.int32)

        @pl.when(there)
        def _():
            pl.semaphore_signal(
                barrier, inc=1, device_id=device(dr, dc), device_id_type=MESH
            )

    for i in (3, 4, 5, 6):
        loads[i].wait()
    wi = w_in[...]
    wi_hi = wi.astype(BF16).astype(F32)
    wi_lo = wi - wi_hi
    bi = b_in[...]
    bi_hi = bi.astype(BF16).astype(F32)
    bi_mid = (bi - bi_hi).astype(BF16).astype(F32)
    bi_lo = bi - bi_hi - bi_mid
    rows8 = lax.broadcasted_iota(jnp.int32, (8, 128), 0)
    bias_rows = jnp.where(
        rows8 == 0, bi_hi, jnp.where(rows8 == 1, bi_mid, jnp.where(rows8 == 2, bi_lo, 0.0))
    )
    stacked = jnp.concatenate(
        [wi_hi, wi_hi, wi_lo, bias_rows, jnp.zeros((96, 128), F32)], axis=0
    )
    lhs1 = stacked.T[:, :32].astype(BF16)
    wide[0:32, :] = w_out[1:33, :]
    wide[32:40, :] = jnp.zeros((8, 128), F32)
    wide[39:40, :] = w_out[0:1, :]
    w40 = wide[0:40, :]
    w40_hi = w40.astype(BF16).astype(F32)
    w40_lo = w40 - w40_hi
    lhs2 = jnp.concatenate(
        [
            jnp.concatenate([w40_hi, w40_hi], axis=1),
            jnp.concatenate([w40_lo, jnp.zeros_like(w40_lo)], axis=1),
        ],
        axis=0,
    ).astype(BF16)
    wide[0:8, :] = jnp.zeros((8, 128), F32)
    wide[0:1, 0:33] = b_out[...]
    bo = pltpu.roll(jnp.broadcast_to(wide[0:1, :], (128, 128)), 127, 1).T
    bo_feat = jnp.concatenate([bo[0:32]] * cw, axis=1)
    bo_dens = jnp.concatenate([bo[127:128]] * cw, axis=1)

    for i in (0, 1):
        loads[i].wait()
    lanes = cw * 128
    ones8 = jnp.ones((8, lanes), F32)
    slot_iota = lax.broadcasted_iota(jnp.int32, (8, lanes), 0)

    def a2a_copy(peer, slot, sem):
        return pltpu.make_async_remote_copy(
            src_ref=send.at[peer],
            dst_ref=recv.at[slot],
            send_sem=a2a_send.at[peer],
            recv_sem=a2a_recv.at[sem],
            device_id={"depth": peer},
            device_id_type=MESH,
        )

    above = n_depth - 1 - depth

    def block_at(i):
        low = jnp.where(i < above, n_depth - 1 - i, i - above)
        high = jnp.where(i < depth, i, n_depth - 1 - i + depth)
        return jnp.where(depth * 2 < n_depth, low, high)

    def block_step(i, carry):
        block = block_at(i)
        parts = []
        for s in range(slots):
            x = jnp.concatenate(
                [
                    vox[
                        pl.ds(
                            s * (chans * n_depth * cw) + block * cw + w,
                            chans,
                            stride=n_depth * cw,
                        ),
                        :,
                    ]
                    for w in range(cw)
                ],
                axis=1,
            )
            x_hi = x.astype(BF16).astype(F32)
            parts.append(
                jnp.concatenate([x_hi, x - x_hi, x_hi, ones8], axis=0).astype(BF16)
            )
        hidden = jnp.maximum(dot(lhs1, jnp.concatenate(parts, axis=1)), 0.0)
        h_hi, h_lo = split(hidden)
        r = dot(lhs2, jnp.concatenate([h_hi, h_lo], axis=0))
        raw = r[0:40] + r[40:80]
        for s in range(slots):
            raw_buf[s] = raw[0:32, s * lanes : (s + 1) * lanes]
            dens[s : s + 1, :] = raw[39:40, s * lanes : (s + 1) * lanes]
        cnt = jnp.concatenate(
            [counts[pl.ds(block * cw + w, 1), :] for w in range(cw)], axis=1
        )
        raw0 = dens[...] + bo_dens
        soft = jnp.maximum(raw0, 0.0) + jnp.log1p(jnp.exp(-jnp.abs(raw0)))
        tau = jnp.where(slot_iota < cnt, soft * step_size, 0.0)
        inc = tau
        for shift in (1, 2, 4):
            inc = inc + jnp.where(slot_iota >= shift, pltpu.roll(inc, shift, 0), 0.0)
        after = jnp.exp(-inc)
        before = jnp.where(slot_iota == 0, 1.0, pltpu.roll(after, 1, 0))
        weight = before - after
        contrib = bo_feat * (1.0 - after[7:8])
        for s in range(slots):
            contrib = contrib + weight[s : s + 1] * raw_buf[s]
        for w in range(cw):
            send[block, w * 32 : (w + 1) * 32, :] = contrib[:, w * 128 : (w + 1) * 128]
        for w in range(cw):
            send[block, 128 + w : 129 + w, :] = inc[7:8, w * 128 : (w + 1) * 128]

        @pl.when(i == 0)
        def _():
            pl.semaphore_wait(barrier, arrivals)

        @pl.when(i < n_depth - 1)
        def _():
            a2a_copy(block, depth, depth).start()

        return carry

    lax.fori_loop(0, n_depth, block_step, 0)
    recv[depth] = send[depth]

    for i in (2, 7, 8, 9, 10):
        loads[i].wait()
    left = lax.broadcasted_iota(jnp.int32, (64, 128), 1) < 64

    def halves(kernels, first, second):
        keep = left[0 : kernels[0].shape[0]]
        zeros = jnp.zeros(keep.shape, F32)
        return split(
            jnp.where(
                keep,
                kernels[first] if 0 <= first <= 2 else zeros,
                kernels[second] if 0 <= second <= 2 else zeros,
            )
        )

    pairs = ((0, 1), (2, 3), (4, -1))
    for b in range(3):
        firsts_k = []
        seconds_k = []
        for a in range(3):
            one = k1[(a * 3 + b) * 32 : (a * 3 + b + 1) * 32, :]
            two = k2[(a * 3 + b) * 64 : (a * 3 + b + 1) * 64, :]
            firsts_k.append(jnp.concatenate([one, one], axis=1))
            seconds_k.append(jnp.concatenate([two, two], axis=1))
        for p, (w0, w1) in enumerate(pairs):
            for position, x in enumerate((0, 1, 2, 3, 4, 5, -2, -1)):
                hi, lo = halves(firsts_k, x - w0 + 1, x - w1 + 1)
                at = (b, pl.ds(position * 32, 32), pl.ds(p * 128, 128))
                t1h[at] = hi
                t1l[at] = lo
            for w in range(4):
                hi, lo = halves(seconds_k, w0 - w + 1, w1 - w + 1)
                at = (b, pl.ds(w * 64, 64), pl.ds(p * 128, 128))
                t2h[at] = hi
                t2l[at] = lo
    bias1 = jnp.concatenate([b1[...]] * 6, axis=1)
    wide[0:1, 0:64] = b2[...]
    bias2 = jnp.broadcast_to(wide[0:1, :], (128, 128)).T[0:64]
    select = (
        lax.broadcasted_iota(jnp.int32, (128, 128), 0) == order[...]
    ).astype(F32).astype(BF16)

    for i, (dr, dc) in enumerate(OFFSETS):
        slot = side.at[(dc + 1) // 2] if dr == 0 else edge.at[(dr + 1) // 2, dc + 1]

        @pl.when(jnp.logical_not(exists(dr, dc)))
        def _():
            slot[...] = jnp.zeros(slot.shape, F32)

    def gather(k, carry):
        before, parts = carry

        @pl.when(k != depth)
        def _():
            a2a_copy(k, k, k).wait_recv()

        fade = jnp.exp(-before)
        parts = tuple(
            parts[w] + fade[w : w + 1] * recv[k, w * 32 : (w + 1) * 32, :]
            for w in range(cw)
        )
        return before + recv[k, 128:136, :], parts

    zero = jnp.zeros((32, 128), F32)
    before, parts = lax.fori_loop(
        0, n_depth, gather, (jnp.zeros((8, 128), F32), (zero,) * cw)
    )
    c_hi, c_lo = split(jnp.concatenate(parts, axis=0))
    image = dot_nt(
        jnp.concatenate([select, select], axis=1), jnp.concatenate([c_hi, c_lo], axis=1)
    )
    own[...] = image

    def halo_copy(i, dr, dc, target=None):
        back = OFFSETS.index((-dr, -dc))
        if dr == 0:
            src, dst = own, side.at[(1 - dc) // 2]
        else:
            src = own.at[0:8] if dr < 0 else own.at[120:128]
            dst = edge.at[(1 - dr) // 2, 1 - dc]
        return pltpu.make_async_remote_copy(
            src_ref=src,
            dst_ref=dst,
            send_sem=halo_send.at[i],
            recv_sem=halo_recv.at[back],
            device_id=device(dr, dc) if target is None else target,
            device_id_type=MESH,
        )

    for i, (dr, dc) in enumerate(OFFSETS):

        @pl.when(exists(dr, dc))
        def _():
            halo_copy(i, dr, dc).start()

    def drain(i, carry):
        a2a_copy((depth + 1 + i) % n_depth, depth, depth).wait_send()
        return carry

    lax.fori_loop(0, n_depth - 1, drain, 0)

    for i, (dr, dc) in enumerate(OFFSETS):

        @pl.when(exists(dr, dc))
        def _():
            j = OFFSETS.index((-dr, -dc))
            halo_copy(j, -dr, -dc, device(dr, dc)).wait_recv()

    lane = lax.broadcasted_iota(jnp.int32, (128, 128), 1)
    pad[8:136, 0:128] = image
    pad[8:136, 128:256] = jnp.where(lane < 64, side[1], side[0])
    pad[0:8, 0:128] = edge[0, 1]
    pad[0:8, 128:256] = jnp.where(lane[0:8] < 64, edge[0, 2], edge[0, 0])
    pad[136:144, 0:128] = edge[1, 1]
    pad[136:144, 128:256] = jnp.where(lane[0:8] < 64, edge[1, 2], edge[1, 0])
    pad[144:152, :] = jnp.zeros((8, 256), F32)

    total = jnp.zeros((144, 384), F32) + bias1
    for b in range(3):
        hi, lo = split(pad[6 + b : 150 + b, :])
        total = total + dot(hi, t1h[b]) + dot(lo, t1h[b]) + dot(hi, t1l[b])
    h = lax.broadcasted_iota(jnp.int32, (144, 384), 0)
    place = lax.broadcasted_iota(jnp.int32, (144, 384), 1) // 64
    outside = (
        ((h == 0) & (row == 0))
        | ((h == 129) & (row == n_row - 1))
        | ((place == 5) & (tile == 0))
        | ((place == 4) & (tile == tiles - 1))
    )
    firsts[...] = jnp.where(outside, 0.0, jnp.maximum(total, 0.0))

    final = jnp.concatenate([bias2] * 4, axis=0)
    for b in range(3):
        hi, lo = split(firsts[b : 128 + b, :])
        final = final + dot_nt(t2h[b], hi) + dot_nt(t2h[b], lo) + dot_nt(t2l[b], hi)
    for w in range(4):
        out[pl.ds(w, 64, stride=4), :] = final[w * 64 : (w + 1) * 64]

    for i, (dr, dc) in enumerate(OFFSETS):

        @pl.when(exists(dr, dc))
        def _():
            halo_copy(i, dr, dc).wait_send()


def on_device(
    voxels,
    counts,
    ray_order,
    weight_in,
    bias_in,
    weight_out,
    bias_out,
    kernel_first,
    bias_first,
    kernel_second,
    bias_second,
):
    slots, chans, n_depth, cw, hb = voxels.shape
    n_row = lax.axis_size("row")
    n_col = lax.axis_size("col")
    step_size = 2.0 / (slots * n_depth)
    out_ch = kernel_second.shape[2]
    sizes = (n_depth, n_row, n_col, slots, chans, step_size)
    vmem = pl.BlockSpec(memory_space=pltpu.VMEM)
    operands = (
        voxels.reshape(slots * chans * n_depth * cw, hb),
        counts.reshape(n_depth * cw, hb),
        ray_order,
        weight_in,
        bias_in.reshape(1, -1),
        weight_out.T,
        bias_out.reshape(1, -1),
        kernel_first.transpose(0, 1, 3, 2).reshape(-1, kernel_first.shape[2]),
        bias_first.reshape(1, -1),
        kernel_second.reshape(-1, kernel_second.shape[3]),
        bias_second.reshape(1, -1),
    )
    out = pl.pallas_call(
        functools.partial(kernel, sizes),
        out_shape=pltpu.VMEM((out_ch * cw, hb), F32),
        in_specs=[pl.BlockSpec(memory_space=pltpu.HBM)] * 11,
        out_specs=vmem,
        scratch_shapes=[pltpu.VMEM(x.shape, x.dtype) for x in operands]
        + [
            pltpu.VMEM((n_depth, 136, 128), F32),
            pltpu.VMEM((n_depth, 136, 128), F32),
            pltpu.VMEM((slots, 32, 512), F32),
            pltpu.VMEM((8, 512), F32),
            pltpu.VMEM((128, 128), F32),
            pltpu.VMEM((2, 128, 128), F32),
            pltpu.VMEM((2, 3, 8, 128), F32),
            pltpu.VMEM((152, 256), F32),
            pltpu.VMEM((144, 384), F32),
            pltpu.VMEM((128, 128), F32),
            pltpu.VMEM((3, 256, 384), BF16),
            pltpu.VMEM((3, 256, 384), BF16),
            pltpu.VMEM((3, 256, 384), BF16),
            pltpu.VMEM((3, 256, 384), BF16),
            pltpu.SemaphoreType.DMA((n_depth,)),
            pltpu.SemaphoreType.DMA((n_depth,)),
            pltpu.SemaphoreType.DMA((8,)),
            pltpu.SemaphoreType.DMA((8,)),
            pltpu.SemaphoreType.DMA((11,)),
        ],
        compiler_params=pltpu.CompilerParams(
            collective_id=0,
            has_side_effects=True,
            vmem_limit_bytes=40000 * 1024,
        ),
    )(*[pltpu.with_memory_space_constraint(x, pltpu.HBM) for x in operands])
    return out.reshape(out_ch, cw, hb)


def solution(mesh):
    in_specs = (
        P("depth", None, None, "col", ("groups", "row")),
        P("depth", None, "col", ("groups", "row")),
        P(("groups", "row"), None),
        P(),
        P(),
        P(),
        P(),
        P(),
        P(),
        P(),
        P(),
    )
    out_specs = P(None, ("depth", "col"), ("groups", "row"))
    return jax.shard_map(
        on_device, mesh=mesh, in_specs=in_specs, out_specs=out_specs, check_vma=False
    )
```
